32 devices in a mesh: groups: 2 (over x), seq: 16 (over z, y, core).
Axes of the slice: x: 2, y: 2, z: 4, core: 2. Of those that a mesh axis runs over, the one named last changes fastest.
Arguments:
- queries: bfloat16 [4, 1024, 1024], P('groups', 'seq'), parts along dimension 0, may hold values from -6 to 6
- keys: bfloat16 [4, 1024, 1024], P('groups', 'seq'), parts along dimension 0, may hold values from -6 to 6
- values: bfloat16 [4, 1024, 1024], P('groups', 'seq'), parts along dimension 0, may hold values from -6 to 6
- resid: bfloat16 [4, 1024, 2048], P('groups', 'seq'), parts along dimension 0, may hold values from -3 to 3
- w_out: bfloat16 [1024, 2048], P('seq'), may hold values from -0.1875 to 0.1875
- w_head: bfloat16 [2048, 256], replicated, may hold values from -0.125 to 0.125
- target: float32 [2048, 256], P(('groups', 'seq')), parts along dimension 0, may hold values from -18 to 18
- block_ids: int32 [2048], P(('groups', 'seq')), parts along dimension 0, may hold values from 0 to 63, never falling along the last dimension, each value on 1 to 32 neighbouring positions
Outputs:
- loss: float32 [2], P('groups'), parts along dimension 0
- d_queries: bfloat16 [4, 1024, 1024], P('groups', 'seq'), parts along dimension 0
- d_keys: bfloat16 [4, 1024, 1024], P('groups', 'seq'), parts along dimension 0
- d_values: bfloat16 [4, 1024, 1024], P('groups', 'seq'), parts along dimension 0
- d_w_out: float32 [2048, 2048], P(('groups', 'seq')), parts along dimension 0
- d_w_head: float32 [4096, 256], P('groups'), parts along dimension 0
The draws below stay inside these ranges and needn't reach their ends.
There are 2 independent parts, one for each index of `groups`. The reference program is written for one: setup_inputs(seed, part) draws one part's arguments, and reference() takes and returns one part's arrays. A program takes and returns all parts, laid end to end along the dimension named above; an argument that names none is the same for every part. Nothing has to cross between parts.
Inputs may be any that keep to these rules, and one draw needn't show every extreme that they name: `block_ids`: never falling along the positions; every block number from 0 to 63 occurs, each block covers 1 to 32 positions and one covers exactly 32. Block 63 borders block 0.
All inputs are finite; a program needn't handle non-finite values.
Results may differ from the reference program's by a relative error of at most 0.0087.
Values may be sent and summed in bfloat16 or wider, within the bound.
A program may use at most 64 MiB of HBM per device.

```python
import math
import jax
import jax.numpy as jnp
import numpy as np
from jax import lax

D = 2048
HEADS = 8
DH = 128
V = 256
MEMBERS = 2
TOK_DEV = 64
HD = 1024
TOKENS = 1024
MOST = 32
COUNT = 64


def draw_queries(key, part):
    key = jax.random.fold_in(key, 11)
    return jnp.clip(jax.random.normal(key, (MEMBERS, TOKENS, HD), jnp.float32), -4.0, 4.0).astype(jnp.bfloat16)


def draw_keys(key, part):
    key = jax.random.fold_in(key, 12)
    return jnp.clip(jax.random.normal(key, (MEMBERS, TOKENS, HD), jnp.float32), -4.0, 4.0).astype(jnp.bfloat16)


def draw_target(key, part):
    key = jax.random.fold_in(key, 13)
    places = jnp.arange(TOKENS).astype(jnp.float32) / (TOKENS - 1)
    rising = 1.0 + 2.0 * places
    return jnp.clip(jax.random.normal(key, (TOKENS, V), jnp.float32), -2.0, 2.0) * rising[:, None]


def levels(rng, extent, shards, least, largest):
    def one(axis_at, blocks):
        heights = jax.random.uniform(jax.random.fold_in(jax.random.fold_in(rng, 6), axis_at), (blocks,), jnp.float32, least / len(shards), largest / len(shards))
        return jnp.repeat(jnp.exp(heights), extent[axis_at] // blocks).reshape((-1,) + (1,) * (len(extent) - axis_at - 1))

    gain = one(*shards[0])
    for cut in shards[1:]:
        gain = gain * one(*cut)
    return gain


def profile(number_of, total, reach, slope):
    portions = [(1 << 20) // math.isqrt(grade ** slope) + 1 for grade in range(2, number_of + 1)]
    spare, holding = total - reach - (number_of - 1), [1] * (number_of - 1)
    while spare > 0:
        free = [i for i in range(number_of - 1) if holding[i] < reach]
        whole, budget = sum([portions[i] for i in free]), spare
        for i in free:
            extra = min(reach - holding[i], max(1, budget * portions[i] // whole), spare)
            holding[i] = holding[i] + extra
            spare = spare - extra
    return np.array([reach] + holding)


def uneven(key, number_of, total, bound, skew):
    if number_of == 2:
        one = jax.random.randint(key, (), max(1, total - bound), min(bound, total - 1) + 1)
        return jnp.stack([one, total - one])
    sizes = jnp.asarray(profile(number_of, total, bound, skew), jnp.int32)
    twos = (number_of - 1) // 2
    giver, receiver = sizes[1:1 + 2 * twos:2], sizes[2:2 + 2 * twos:2]
    margin = jnp.minimum(giver - 1, bound - receiver)
    moved = jax.random.randint(jax.random.fold_in(key, 1), (twos,), 0, 1 << 20) % (margin + 1)
    sizes = sizes.at[1:1 + 2 * twos:2].set(giver - moved).at[2:2 + 2 * twos:2].set(receiver + moved)
    return sizes[jax.random.permutation(jax.random.fold_in(key, 2), number_of)]


def gaussian(stream_key, shape, width, limit, split=(), kind=jnp.bfloat16):
    values = width * jax.random.normal(stream_key, shape, jnp.float32)
    if split:
        values = values * levels(stream_key, shape, split, -0.22, 0.18)
    return jnp.clip(values, -limit, limit).astype(kind)


def setup_inputs(seed: int = 0, part: int = 0) -> dict:
    key_list = jax.random.split(jax.random.key(seed), 9)
    part_splits = jax.random.split(jax.random.fold_in(key_list[8], part), 9)
    queries = draw_queries(jax.random.fold_in(jax.random.fold_in(key_list[8], part), 71), part)
    keys = draw_keys(jax.random.fold_in(jax.random.fold_in(key_list[8], part), 71), part)
    values = gaussian(part_splits[2], (MEMBERS, TOKENS, HD), 1.0, 6.0, ((1, 16),))
    resid = gaussian(part_splits[3], (MEMBERS, TOKENS, D), 0.5, 3.0, ((1, 16),))
    w_out = gaussian(key_list[4], (HD, D), HD ** -0.5, 0.1875, ((0, 16),))
    w_head = gaussian(key_list[5], (D, V), D ** -0.5, 0.125)
    target = draw_target(jax.random.fold_in(jax.random.fold_in(key_list[8], part), 71), part)
    block_ids = jnp.searchsorted(jnp.cumsum(uneven(part_splits[7], COUNT, TOKENS, MOST, 1)), jnp.arange(TOKENS), side="right").astype(jnp.int32)
    return dict(queries=queries, keys=keys, values=values, resid=resid, w_out=w_out, w_head=w_head, target=target, block_ids=block_ids)


def link_mask(query_ids, key_ids, number):
    gap = (query_ids[:, None] - key_ids[None, :]) % number
    return (gap == 0) | (gap == 1) | (gap == number - 1)

def ensemble_score(predicted, target):
    members = predicted.shape[0]
    offset_t = predicted - target[None]
    soft = jnp.sqrt(1.0 + offset_t * offset_t)
    pairwise = predicted[:, None] - predicted[None, :]
    soft_pair = jnp.sqrt(1.0 + pairwise * pairwise)
    score = jnp.sum(soft - 1.0) / members - jnp.sum(soft_pair - 1.0) / (2 * members * (members - 1))
    gradient = offset_t / soft / members - lax.optimization_barrier(jnp.sum(pairwise / soft_pair, axis=1)) / (members * (members - 1))
    return (score, gradient)

def attention_weights(query_part, key_part, allowed):
    scores = jnp.einsum('qhd,khd->hqk', query_part.astype(jnp.float32), key_part.astype(jnp.float32)) * DH ** (-0.5)
    scores = jnp.where(allowed[None], scores, -1e+30)
    peak = lax.optimization_barrier(jnp.max(scores, axis=-1, keepdims=True))
    exponent = jnp.exp(scores - peak)
    probs = exponent / lax.optimization_barrier(jnp.sum(exponent, axis=-1, keepdims=True))
    probs_half = lax.optimization_barrier(probs.astype(jnp.bfloat16))
    return (probs, probs_half)

def attend_forward(query_part, key_part, value_part, allowed):
    probs, probs_half = attention_weights(query_part, key_part, allowed)
    return jnp.einsum('hqk,khd->qhd', probs_half.astype(jnp.float32), value_part.astype(jnp.float32)).astype(jnp.bfloat16)

def attend_backward(query_part, key_part, value_part, grad_part, allowed):
    probs, probs_half = attention_weights(query_part, key_part, allowed)
    d_probs = jnp.einsum('qhd,khd->hqk', grad_part.astype(jnp.float32), value_part.astype(jnp.float32))
    delta = lax.optimization_barrier(jnp.sum(probs * d_probs, axis=-1, keepdims=True))
    d_scores = lax.optimization_barrier((probs * (d_probs - delta) * DH ** (-0.5)).astype(jnp.bfloat16))
    d_query = jnp.einsum('hqk,khd->qhd', d_scores.astype(jnp.float32), key_part.astype(jnp.float32)).astype(jnp.bfloat16)
    d_key = jnp.einsum('hqk,qhd->khd', d_scores.astype(jnp.float32), query_part.astype(jnp.float32))
    d_value = jnp.einsum('hqk,qhd->khd', probs_half.astype(jnp.float32), grad_part.astype(jnp.float32))
    return (d_query, d_key, d_value)

def reference(queries, keys, values, resid, w_out, w_head, target, block_ids):
    blocks = TOKENS // TOK_DEV
    span = 3 * TOK_DEV

    def extend(array):
        return jnp.concatenate([array[:, TOKENS - TOK_DEV:], array, array[:, :TOK_DEV]], axis=1)
    keys_ext = extend(keys)
    values_ext = extend(values)
    ids_ext = jnp.concatenate([block_ids[TOKENS - TOK_DEV:], block_ids, block_ids[:TOK_DEV]])

    def block_inputs(index):
        offset = index * TOK_DEV
        query_rows = lax.dynamic_slice_in_dim(queries, offset, TOK_DEV, 1).reshape(MEMBERS, TOK_DEV, HEADS, DH)
        key_rows = lax.dynamic_slice_in_dim(keys_ext, offset, span, 1).reshape(MEMBERS, span, HEADS, DH)
        value_rows = lax.dynamic_slice_in_dim(values_ext, offset, span, 1).reshape(MEMBERS, span, HEADS, DH)
        allowed = link_mask(lax.dynamic_slice_in_dim(block_ids, offset, TOK_DEV, 0), lax.dynamic_slice_in_dim(ids_ext, offset, span, 0), COUNT)
        return (query_rows, key_rows, value_rows, allowed)

    def forward_block(index):
        query_rows, key_rows, value_rows, allowed = block_inputs(index)
        attended = jax.vmap(lambda qpart, kpart, vpart: attend_forward(qpart, kpart, vpart, allowed))(query_rows, key_rows, value_rows)
        return attended.reshape(MEMBERS, TOK_DEV, HD)
    attn = lax.map(forward_block, jnp.arange(blocks, dtype=jnp.int32))
    attn = jnp.transpose(attn, (1, 0, 2, 3)).reshape(MEMBERS, TOKENS, HD)
    attn_flat = attn.reshape(MEMBERS * TOKENS, HD)
    projected = jnp.dot(attn_flat, w_out, preferred_element_type=jnp.float32)
    mixed = (resid.reshape(MEMBERS * TOKENS, D).astype(jnp.float32) + projected).astype(jnp.bfloat16)
    predicted = jnp.dot(mixed, w_head, preferred_element_type=jnp.float32).reshape(MEMBERS, TOKENS, V)
    score, gradient = ensemble_score(predicted, target)
    loss = (score / (TOKENS * V)).reshape(1)
    d_pred = gradient.astype(jnp.bfloat16).reshape(MEMBERS * TOKENS, V)
    d_w_head = jnp.dot(mixed.T, d_pred, preferred_element_type=jnp.float32)
    d_mixed = jnp.dot(d_pred, w_head.T, preferred_element_type=jnp.float32).astype(jnp.bfloat16)
    attended_pred = jnp.dot(attn_flat.T, d_pred, preferred_element_type=jnp.float32)
    d_w_out = jnp.dot(attended_pred, w_head.astype(jnp.float32).T, precision=lax.Precision.HIGHEST)
    d_attn = jnp.dot(d_mixed, w_out.T, preferred_element_type=jnp.float32).astype(jnp.bfloat16).reshape(MEMBERS, TOKENS, HD)

    def backward_block(index):
        query_rows, key_rows, value_rows, allowed = block_inputs(index)
        grad_rows = lax.dynamic_slice_in_dim(d_attn, index * TOK_DEV, TOK_DEV, 1).reshape(MEMBERS, TOK_DEV, HEADS, DH)
        d_query, d_key, d_value = jax.vmap(lambda qpart, kpart, vpart, gpart: attend_backward(qpart, kpart, vpart, gpart, allowed))(query_rows, key_rows, value_rows, grad_rows)
        return (d_query.reshape(MEMBERS, TOK_DEV, HD), d_key.reshape(MEMBERS, span, HD), d_value.reshape(MEMBERS, span, HD))
    d_q_blocks, d_k_blocks, d_v_blocks = lax.map(backward_block, jnp.arange(blocks, dtype=jnp.int32))
    d_queries = jnp.transpose(d_q_blocks, (1, 0, 2, 3)).reshape(MEMBERS, TOKENS, HD)

    def assemble(parts):
        middle = parts[:, :, TOK_DEV:2 * TOK_DEV]
        from_next = jnp.roll(parts[:, :, :TOK_DEV], -1, axis=0)
        from_prior = jnp.roll(parts[:, :, 2 * TOK_DEV:], 1, axis=0)
        combined = (middle + from_next + from_prior).astype(jnp.bfloat16)
        return jnp.transpose(combined, (1, 0, 2, 3)).reshape(MEMBERS, TOKENS, HD)
    return (loss, d_queries, assemble(d_k_blocks), assemble(d_v_blocks), d_w_out, d_w_head)
```

```python
import functools

import jax
import jax.numpy as jnp
from jax import lax
from jax.experimental import pallas as pl
from jax.experimental.pallas import tpu as pltpu
from jax.sharding import PartitionSpec as P

DH = 128
F32 = jnp.float32
BF16 = jnp.bfloat16


def dot_nn(a, b):
    return lax.dot_general(a, b, (((1,), (0,)), ((), ())), preferred_element_type=F32)


def dot_nt(a, b, precision=None):
    return lax.dot_general(
        a, b, (((1,), (1,)), ((), ())), preferred_element_type=F32, precision=precision
    )


def dot_tn(a, b):
    return lax.dot_general(a, b, (((0,), (0,)), ((), ())), preferred_element_type=F32)


def kernel(
    n,
    q, k, v, resid, w_out, w_head, target, ids,
    loss_o, dq_o, dk_o, dv_o, dwo_o, dwh_o,
    kw, vw, qw, idw, dpw, stw,
    m_all, pred0, bias, probs, att, dpred, da, stats, stats_t,
    ap_f, ap_b, ap_r1, ap_s2, ap_r2,
    g_f, g_b, g_r1, g_s2, g_r2,
    loss_own, loss_sib, loss_all,
    halo_ss, halo_rs, m_ss, m_rs, sib_ss, sib_rs, ap_ss, ap_rs, g_ss, g_rs,
    ag_ss, ag_rs, fw_ss, fw_rs, lo_ss, lo_rs,
):
    members, tok, hd = q.shape
    heads = hd // DH
    dm = resid.shape[2]
    nc = n // 2
    ar = hd // n
    gr = dm // n
    scaling = DH ** (-0.5)
    me = lax.axis_index("seq")
    chip, par = me // 2, me % 2
    sib = chip * 2 + (1 - par)
    left, right = lax.rem(me + n - 1, n), lax.rem(me + 1, n)
    outer = lax.rem(me + n - 1 + 2 * par, n)

    def peer_chip(off):
        return lax.rem(chip + off, nc)

    def source_chip(off):
        return lax.rem(chip + nc - off, nc)

    def remote(src, dst, ss, rs, to):
        copy = pltpu.make_async_remote_copy(
            src_ref=src, dst_ref=dst, send_sem=ss, recv_sem=rs,
            device_id={"seq": to}, device_id_type=pl.DeviceIdType.MESH,
        )
        copy.start()
        return copy

    barrier = pltpu.get_barrier_semaphore()
    for to in [sib, outer] + [peer_chip(off) * 2 + par for off in range(1, nc)]:
        pl.semaphore_signal(
            barrier, inc=1, device_id={"seq": to}, device_id_type=pl.DeviceIdType.MESH
        )
    pl.semaphore_wait(barrier, nc + 1)

    pending = []

    def halo(slot, src, dst):
        pair = (
            remote(src, dst.at[0], halo_ss.at[2 * slot], halo_rs.at[2 * slot], right),
            remote(src, dst.at[1], halo_ss.at[2 * slot + 1], halo_rs.at[2 * slot + 1], left),
        )
        pending.extend(pair)
        return pair

    halo_id = halo(0, ids, idw)
    halo_k = halo(1, k, kw)
    halo_v = halo(2, v, vw)

    m_all[chip, par] = dot_nn(w_out[...], w_head[...]).astype(BF16)
    m_copies = [
        remote(m_all.at[chip, par], m_all.at[chip, par], m_ss.at[off], m_rs.at[off],
               peer_chip(off) * 2 + par)
        for off in range(1, nc)
    ]
    pending.extend(m_copies)
    halo_q = halo(3, q, qw)

    pred0[...] = dot_nn(resid[...].reshape(members * tok, dm), w_head[...])

    for copy in halo_id + halo_k:
        copy.wait_recv()
    id_window = jnp.concatenate([idw[0], ids[...], idw[1]], axis=0)
    lane = lax.broadcasted_iota(jnp.int32, (tok, DH), 1)
    first = jnp.where(lane == 0, 1.0, 0.0).astype(BF16)
    window_ids = dot_nt(first, id_window)
    own_ids = ids[...].astype(F32)[:, 0:1]
    gap = jnp.abs(own_ids - window_ids)
    number = 4.0 * n
    bias[...] = jnp.where((gap < 1.5) | (gap > number - 1.5), 0.0, -1e30)

    def cols(h):
        return pl.ds(pl.multiple_of(h * DH, DH), DH)

    def window(side, own, m, h):
        return jnp.concatenate(
            [side[0, m, :, cols(h)], own[m, :, cols(h)], side[1, m, :, cols(h)]], axis=0
        )

    unroll = 2

    def softmax_step(step, held):
        for u in range(unroll):
            h = step * unroll + u
            for m in range(members):
                c = m * heads + h
                s = dot_nt(q[m, :, cols(h)], window(kw, k, m, h)) * scaling + bias[...]
                peak = jnp.max(s, axis=-1, keepdims=True)
                e = jnp.exp(s - peak)
                total = jnp.sum(e, axis=-1, keepdims=True)
                probs[c] = e / total
                held = jnp.where(lane == c, peak + jnp.log(total), held)
        return held

    lse = lax.fori_loop(0, heads // unroll, softmax_step, jnp.zeros((tok, DH), F32))

    for copy in m_copies:
        copy.wait_recv()
    m_forward = remote(m_all.at[:, par], m_all.at[:, par], sib_ss.at[0], sib_rs.at[0], sib)
    pending.append(m_forward)
    for copy in halo_v:
        copy.wait_recv()

    def attend_step(step, _):
        for u in range(unroll):
            h = step * unroll + u
            for m in range(members):
                p = probs[m * heads + h].astype(BF16)
                att[m, :, cols(h)] = dot_nn(p, window(vw, v, m, h)).astype(BF16)
        return 0

    lax.fori_loop(0, heads // unroll, attend_step, 0)

    m_forward.wait_recv()
    attended = att[...].reshape(members * tok, hd)
    m_full = m_all[...].reshape(hd, -1)
    predicted = pred0[...] + dot_nn(attended, m_full)
    p0, p1 = predicted[:tok], predicted[tok:]
    o0, o1, pair = p0 - target[...], p1 - target[...], p0 - p1
    s0 = jnp.sqrt(1.0 + o0 * o0)
    s1 = jnp.sqrt(1.0 + o1 * o1)
    sp = jnp.sqrt(1.0 + pair * pair)
    score = 0.5 * ((s0 - 1.0) + (s1 - 1.0)) - 0.5 * (sp - 1.0)
    shared = 0.5 * (pair / sp)
    dpred[0:tok] = (0.5 * (o0 / s0) - shared).astype(BF16)
    dpred[tok:] = (0.5 * (o1 / s1) + shared).astype(BF16)
    halo_d = halo(4, dpred, dpw)

    step_rows = 256
    per = step_rows // (2 * ar)
    for i in range(hd // step_rows):
        part = dot_tn(attended[:, i * step_rows:(i + 1) * step_rows], dpred[...])
        part = part.reshape(per, 2, ar, -1)
        ap_f[i * per:(i + 1) * per] = part
        ap_b[i * per:(i + 1) * per] = part.astype(BF16)
    ap_pair = remote(ap_b.at[:, 1 - par], ap_r1, sib_ss.at[1], sib_rs.at[1], sib)
    pending.append(ap_pair)

    loss_own[...] = jnp.broadcast_to(jnp.sum(score).reshape(1, 1), loss_own.shape)
    loss_pair = remote(loss_own, loss_sib, sib_ss.at[2], sib_rs.at[2], sib)
    pending.append(loss_pair)

    da[1] = dot_nt(dpred[...], m_full).astype(BF16).reshape(members, tok, hd)

    ap_pair.wait_recv()
    ap_copies = []
    for off in range(1, nc):
        c = peer_chip(off)
        ap_s2[c] = (ap_f[c, par] + ap_r1[c].astype(F32)).astype(BF16)
        ap_copies.append(
            remote(ap_s2.at[c], ap_r2.at[off], ap_ss.at[off], ap_rs.at[off], c * 2 + par)
        )
    pending.extend(ap_copies)
    loss_pair.wait_recv()
    loss_all[chip] = loss_own[...] + loss_sib[...]
    loss_copies = [
        remote(loss_all.at[chip], loss_all.at[chip], lo_ss.at[off], lo_rs.at[off],
               peer_chip(off) * 2 + par)
        for off in range(1, nc)
    ]
    pending.extend(loss_copies)

    gper = step_rows // (2 * gr)
    rows = resid[...].reshape(members * tok, dm)
    for i in range(dm // step_rows):
        part = dot_tn(rows[:, i * step_rows:(i + 1) * step_rows], dpred[...])
        g_f[i * gper:(i + 1) * gper] = part.reshape(gper, 2, gr, -1)

    def query_grad_step(step, held):
        for u in range(unroll):
            h = step * unroll + u
            for m in range(members):
                c = m * heads + h
                p = probs[c]
                dp = dot_nt(da[1, m, :, cols(h)], window(vw, v, m, h))
                delta = jnp.sum(p * dp, axis=-1, keepdims=True)
                ds = (p * (dp - delta) * scaling).astype(BF16)
                dq_o[m, :, cols(h)] = dot_nn(ds, window(kw, k, m, h)).astype(BF16)
                held = jnp.where(lane == members * heads + c, delta, held)
        return held

    stats[...] = lax.fori_loop(0, heads // unroll, query_grad_step, lse)
    halo_s = halo(5, stats, stw)

    for copy in ap_copies:
        copy.wait_recv()
    ap_total = ap_f[chip, par] + ap_r1[chip].astype(F32)
    for off in range(1, nc):
        ap_total = ap_total + ap_r2[off].astype(F32)
    ap_high = ap_total.astype(BF16)
    for i in range(dm // step_rows):
        part = dot_tn(w_out[:, i * step_rows:(i + 1) * step_rows], ap_high)
        part = g_f[i * gper:(i + 1) * gper] + part.reshape(gper, 2, gr, -1)
        g_f[i * gper:(i + 1) * gper] = part
        g_b[i * gper:(i + 1) * gper] = part.astype(BF16)
    g_pair = remote(g_b.at[:, 1 - par], g_r1, sib_ss.at[3], sib_rs.at[3], sib)
    pending.append(g_pair)
    ap_low = (ap_total - ap_high.astype(F32)).astype(BF16)
    dwo_o[...] = dot_nt(ap_high, w_head[...]) + dot_nt(ap_low, w_head[...])
    g_pair.wait_recv()
    g_copies = []
    for off in range(1, nc):
        c = peer_chip(off)
        g_s2[c] = (g_f[c, par] + g_r1[c].astype(F32)).astype(BF16)
        g_copies.append(
            remote(g_s2.at[c], g_r2.at[off], g_ss.at[off], g_rs.at[off], c * 2 + par)
        )
    pending.extend(g_copies)

    for copy in halo_d:
        copy.wait_recv()
    for side, place in ((0, 0), (1, 2)):
        da[place] = dot_nt(dpw[side], m_full).astype(BF16).reshape(members, tok, hd)
    for copy in halo_q + halo_s:
        copy.wait_recv()
    stat_window = jnp.concatenate([stw[0], stats[...], stw[1]], axis=0)
    count = stats_t.shape[0]
    eye = jnp.where(
        lax.broadcasted_iota(jnp.int32, (count, DH), 0)
        == lax.broadcasted_iota(jnp.int32, (count, DH), 1), 1.0, 0.0
    )
    stats_t[...] = dot_nt(eye, stat_window, lax.Precision.HIGHEST)

    def key_grad_step(step, _):
        for u in range(unroll):
            h = step * unroll + u
            for m in range(members):
                c = m * heads + h
                queries = window(qw, q, m, h)
                grads = jnp.concatenate([da[i, m, :, cols(h)] for i in range(3)], axis=0)
                s = dot_nt(k[m, :, cols(h)], queries) * scaling + bias[...]
                p = jnp.exp(s - stats_t[pl.ds(c, 1), :])
                dp = dot_nt(v[m, :, cols(h)], grads)
                ds = (p * (dp - stats_t[pl.ds(members * heads + c, 1), :]) * scaling).astype(BF16)
                dv_o[m, :, cols(h)] = dot_nn(p.astype(BF16), grads).astype(BF16)
                dk_o[m, :, cols(h)] = dot_nn(ds, queries).astype(BF16)
        return 0

    lax.fori_loop(0, heads // unroll, key_grad_step, 0)

    for copy in g_copies:
        copy.wait_recv()
    g_total = g_f[chip, par] + g_r1[chip].astype(F32)
    for off in range(1, nc):
        g_total = g_total + g_r2[off].astype(F32)
    dwh_o[chip, par] = g_total.astype(BF16)
    ag_copies = [
        remote(dwh_o.at[chip, par], dwh_o.at[chip, par], ag_ss.at[off], ag_rs.at[off],
               peer_chip(off) * 2 + par)
        for off in range(1, nc)
    ]
    pending.extend(ag_copies)
    forwards = [remote(dwh_o.at[chip, par], dwh_o.at[chip, par], fw_ss.at[0], fw_rs.at[0], sib)]
    for copy in loss_copies:
        copy.wait_recv()
    loss_o[...] = jnp.sum(loss_all[...], axis=0)
    for off in range(1, nc):
        ag_copies[off - 1].wait_recv()
        c = source_chip(off)
        forwards.append(
            remote(dwh_o.at[c, par], dwh_o.at[c, par], fw_ss.at[off], fw_rs.at[off], sib)
        )
    for copy in forwards:
        copy.wait_recv()
    for copy in pending + forwards:
        copy.wait_send()


def per_device(queries, keys, values, resid, w_out, w_head, target, block_ids):
    members, tok, hd = queries.shape
    heads = hd // DH
    n = lax.axis_size("seq")
    nc = n // 2
    dm, width = w_head.shape
    ar, gr = hd // n, dm // n
    ids = jnp.broadcast_to(block_ids.astype(BF16)[:, None], (tok, DH))
    vm = pl.BlockSpec(memory_space=pltpu.VMEM)
    dma = pltpu.SemaphoreType.DMA
    like = jax.ShapeDtypeStruct(queries.shape, BF16)
    loss, d_queries, d_keys, d_values, d_w_out, d_w_head = pl.pallas_call(
        functools.partial(kernel, n),
        out_shape=(
            jax.ShapeDtypeStruct((8, DH), F32),
            like, like, like,
            jax.ShapeDtypeStruct((ar, dm), F32),
            jax.ShapeDtypeStruct((nc, 2, gr, width), BF16),
        ),
        in_specs=[vm] * 8,
        out_specs=(vm,) * 6,
        scratch_shapes=[
            pltpu.VMEM((2,) + keys.shape, BF16),
            pltpu.VMEM((2,) + keys.shape, BF16),
            pltpu.VMEM((2,) + keys.shape, BF16),
            pltpu.VMEM((2, tok, DH), BF16),
            pltpu.VMEM((2, members * tok, width), BF16),
            pltpu.VMEM((2, tok, DH), F32),
            pltpu.VMEM((nc, 2, ar, width), BF16),
            pltpu.VMEM((members * tok, width), F32),
            pltpu.VMEM((tok, 3 * tok), F32),
            pltpu.VMEM((members * heads, tok, 3 * tok), F32),
            pltpu.VMEM(queries.shape, BF16),
            pltpu.VMEM((members * tok, width), BF16),
            pltpu.VMEM((3,) + queries.shape, BF16),
            pltpu.VMEM((tok, DH), F32),
            pltpu.VMEM((2 * members * heads, 3 * tok), F32),
            pltpu.VMEM((nc, 2, ar, width), F32),
            pltpu.VMEM((nc, 2, ar, width), BF16),
            pltpu.VMEM((nc, ar, width), BF16),
            pltpu.VMEM((nc, ar, width), BF16),
            pltpu.VMEM((nc, ar, width), BF16),
            pltpu.VMEM((nc, 2, gr, width), F32),
            pltpu.VMEM((nc, 2, gr, width), BF16),
            pltpu.VMEM((nc, gr, width), BF16),
            pltpu.VMEM((nc, gr, width), BF16),
            pltpu.VMEM((nc, gr, width), BF16),
            pltpu.VMEM((8, DH), F32),
            pltpu.VMEM((8, DH), F32),
            pltpu.VMEM((nc, 8, DH), F32),
            dma((12,)), dma((12,)),
            dma((nc,)), dma((nc,)),
            dma((4,)), dma((4,)),
            dma((nc,)), dma((nc,)),
            dma((nc,)), dma((nc,)),
            dma((nc,)), dma((nc,)),
            dma((nc,)), dma((nc,)),
            dma((nc,)), dma((nc,)),
        ],
        compiler_params=pltpu.CompilerParams(
            collective_id=0, has_side_effects=True, vmem_limit_bytes=48 * 1024 * 1024
        ),
        cost_estimate=pl.CostEstimate(
            flops=2_000_000_000, bytes_accessed=6_000_000, transcendentals=1_000_000
        ),
    )(queries, keys, values, resid, w_out, w_head, target, ids)
    loss = (loss[0, 0] / (n * tok * width)).reshape(1)
    return (
        loss, d_queries, d_keys, d_values, d_w_out,
        d_w_head.reshape(dm, width).astype(F32),
    )


def solution(mesh):
    return jax.shard_map(
        per_device,
        mesh=mesh,
        in_specs=(
            P("groups", "seq", None),
            P("groups", "seq", None),
            P("groups", "seq", None),
            P("groups", "seq", None),
            P("seq", None),
            P(),
            P(("groups", "seq"), None),
            P(("groups", "seq")),
        ),
        out_specs=(
            P("groups"),
            P("groups", "seq", None),
            P("groups", "seq", None),
            P("groups", "seq", None),
            P(("groups", "seq"), None),
            P("groups", None),
        ),
        check_vma=False,
    )
```

```python
import functools

import jax
import jax.numpy as jnp
from jax import lax
from jax.experimental import pallas as pl
from jax.experimental.pallas import tpu as pltpu
from jax.sharding import PartitionSpec as P

DH = 128
F32 = jnp.float32
BF16 = jnp.bfloat16


def dot_nn(a, b):
    return lax.dot_general(a, b, (((1,), (0,)), ((), ())), preferred_element_type=F32)


def dot_nt(a, b, precision=None):
    return lax.dot_general(
        a, b, (((1,), (1,)), ((), ())), preferred_element_type=F32, precision=precision
    )


def dot_tn(a, b):
    return lax.dot_general(a, b, (((0,), (0,)), ((), ())), preferred_element_type=F32)


def kernel(
    n,
    q_in, k_in, v_in, resid_in, w_out_in, w_head_in, target_in, ids_in,
    loss_out, dq_out, dk_out, dv_out, dwo_out, dwh_out,
    loss_o, dq_o, dk_o, dv_o, dwo_o, dwh_o, out_sem,
    q, k, v, resid, w_out, w_head, target, id_row, ids, in_sem,
    kw, vw, qw, idw, dpw, stw,
    m_all, pred0, bias, probs, att, dpred, da, stats, stats_t,
    ap_f, ap_b, ap_r1, ap_s2, ap_r2,
    g_f, g_b, g_r1, g_s2, g_r2,
    loss_own, loss_sib, loss_all,
    halo_ss, halo_rs, m_ss, m_rs, sib_ss, sib_rs, ap_ss, ap_rs, g_ss, g_rs,
    ag_ss, ag_rs, fw_ss, fw_rs, lo_ss, lo_rs,
):
    members, tok, hd = q.shape
    heads = hd // DH
    dm = resid.shape[2]
    nc = n // 2
    ar = hd // n
    gr = dm // n
    scaling = DH ** (-0.5)
    me = lax.axis_index("seq")
    chip, par = me // 2, me % 2
    sib = chip * 2 + (1 - par)
    left, right = lax.rem(me + n - 1, n), lax.rem(me + 1, n)
    outer = lax.rem(me + n - 1 + 2 * par, n)

    def peer_chip(off):
        return lax.rem(chip + off, nc)

    def source_chip(off):
        return lax.rem(chip + nc - off, nc)

    def remote(src, dst, ss, rs, to):
        copy = pltpu.make_async_remote_copy(
            src_ref=src, dst_ref=dst, send_sem=ss, recv_sem=rs,
            device_id={"seq": to}, device_id_type=pl.DeviceIdType.MESH,
        )
        copy.start()
        return copy

    local = [
        pltpu.make_async_copy(src, dst, in_sem.at[i])
        for i, (src, dst) in enumerate((
            (ids_in, id_row), (w_head_in, w_head), (w_out_in, w_out), (k_in, k), (resid_in, resid),
            (q_in, q), (v_in, v), (target_in, target),
        ))
    ]
    for copy in local:
        copy.start()

    written = []

    def write(src, dst):
        copy = pltpu.make_async_copy(src, dst, out_sem.at[len(written)])
        copy.start()
        written.append(copy)

    barrier = pltpu.get_barrier_semaphore()
    for to in [sib, outer] + [peer_chip(off) * 2 + par for off in range(1, nc)]:
        pl.semaphore_signal(
            barrier, inc=1, device_id={"seq": to}, device_id_type=pl.DeviceIdType.MESH
        )
    local[0].wait()
    square = (tok, tok)
    diagonal = lax.broadcasted_iota(jnp.int32, square, 0) == lax.broadcasted_iota(jnp.int32, square, 1)
    id_column = jnp.sum(
        jnp.where(diagonal, id_row[...].astype(F32), 0.0), axis=1, keepdims=True
    )
    ids[...] = jnp.broadcast_to(id_column, ids.shape).astype(BF16)
    pl.semaphore_wait(barrier, nc + 1)

    pending = []

    def halo(slot, src, dst):
        pair = (
            remote(src, dst.at[0], halo_ss.at[2 * slot], halo_rs.at[2 * slot], right),
            remote(src, dst.at[1], halo_ss.at[2 * slot + 1], halo_rs.at[2 * slot + 1], left),
        )
        pending.extend(pair)
        return pair

    halo_id = halo(0, ids, idw)
    halo_k = halo(1, k_in, kw)
    halo_v = halo(2, v_in, vw)
    local[1].wait()
    local[2].wait()

    m_all[chip, par] = dot_nn(w_out[...], w_head[...]).astype(BF16)
    m_copies = [
        remote(m_all.at[chip, par], m_all.at[chip, par], m_ss.at[off], m_rs.at[off],
               peer_chip(off) * 2 + par)
        for off in range(1, nc)
    ]
    pending.extend(m_copies)
    for copy in local[3:]:
        copy.wait()

    pred0[...] = dot_nn(resid[...].reshape(members * tok, dm), w_head[...])

    for copy in halo_id + halo_k:
        copy.wait_recv()
    id_window = jnp.concatenate([idw[0], ids[...], idw[1]], axis=0)
    lane = lax.broadcasted_iota(jnp.int32, (tok, DH), 1)
    first = jnp.where(lane == 0, 1.0, 0.0).astype(BF16)
    window_ids = dot_nt(first, id_window)
    own_ids = ids[...].astype(F32)[:, 0:1]
    gap = jnp.abs(own_ids - window_ids)
    number = 4.0 * n
    bias[...] = jnp.where((gap < 1.5) | (gap > number - 1.5), 0.0, -1e30)

    def cols(h):
        return pl.ds(pl.multiple_of(h * DH, DH), DH)

    def window(side, own, m, h):
        return jnp.concatenate(
            [side[0, m, :, cols(h)], own[m, :, cols(h)], side[1, m, :, cols(h)]], axis=0
        )

    unroll = 2

    def softmax_step(step, held):
        for u in range(unroll):
            h = step * unroll + u
            for m in range(members):
                c = m * heads + h
                s = dot_nt(q[m, :, cols(h)], window(kw, k, m, h)) * scaling + bias[...]
                peak = jnp.max(s, axis=-1, keepdims=True)
                e = jnp.exp(s - peak)
                total = jnp.sum(e, axis=-1, keepdims=True)
                probs[c] = e / total
                held = jnp.where(lane == c, peak + jnp.log(total), held)
        return held

    lse = lax.fori_loop(0, heads // unroll, softmax_step, jnp.zeros((tok, DH), F32))

    for copy in m_copies:
        copy.wait_recv()
    m_forward = remote(m_all.at[:, par], m_all.at[:, par], sib_ss.at[0], sib_rs.at[0], sib)
    pending.append(m_forward)
    for copy in halo_v:
        copy.wait_recv()
    halo_q = halo(3, q_in, qw)

    def attend_step(step, _):
        for u in range(unroll):
            h = step * unroll + u
            for m in range(members):
                p = probs[m * heads + h].astype(BF16)
                att[m, :, cols(h)] = dot_nn(p, window(vw, v, m, h)).astype(BF16)
        return 0

    lax.fori_loop(0, heads // unroll, attend_step, 0)

    m_forward.wait_recv()
    attended = att[...].reshape(members * tok, hd)
    m_full = m_all[...].reshape(hd, -1)
    predicted = pred0[...] + dot_nn(attended, m_full)
    p0, p1 = predicted[:tok], predicted[tok:]
    o0, o1, pair = p0 - target[...], p1 - target[...], p0 - p1
    s0 = jnp.sqrt(1.0 + o0 * o0)
    s1 = jnp.sqrt(1.0 + o1 * o1)
    sp = jnp.sqrt(1.0 + pair * pair)
    score = 0.5 * ((s0 - 1.0) + (s1 - 1.0)) - 0.5 * (sp - 1.0)
    shared = 0.5 * (pair / sp)
    dpred[0:tok] = (0.5 * (o0 / s0) - shared).astype(BF16)
    dpred[tok:] = (0.5 * (o1 / s1) + shared).astype(BF16)
    halo_d = halo(4, dpred, dpw)

    step_rows = 256
    per = step_rows // (2 * ar)
    for i in range(hd // step_rows):
        part = dot_tn(attended[:, i * step_rows:(i + 1) * step_rows], dpred[...])
        part = part.reshape(per, 2, ar, -1)
        ap_f[i * per:(i + 1) * per] = part
        ap_b[i * per:(i + 1) * per] = part.astype(BF16)
    ap_pair = remote(ap_b.at[:, 1 - par], ap_r1, sib_ss.at[1], sib_rs.at[1], sib)
    pending.append(ap_pair)

    loss_own[...] = jnp.broadcast_to(jnp.sum(score).reshape(1, 1), loss_own.shape)
    loss_pair = remote(loss_own, loss_sib, sib_ss.at[2], sib_rs.at[2], sib)
    pending.append(loss_pair)

    da[1] = dot_nt(dpred[...], m_full).astype(BF16).reshape(members, tok, hd)

    ap_pair.wait_recv()
    ap_copies = []
    for off in range(1, nc):
        c = peer_chip(off)
        ap_s2[c] = (ap_f[c, par] + ap_r1[c].astype(F32)).astype(BF16)
        ap_copies.append(
            remote(ap_s2.at[c], ap_r2.at[off], ap_ss.at[off], ap_rs.at[off], c * 2 + par)
        )
    pending.extend(ap_copies)
    loss_pair.wait_recv()
    loss_all[chip] = loss_own[...] + loss_sib[...]
    loss_copies = [
        remote(loss_all.at[chip], loss_all.at[chip], lo_ss.at[off], lo_rs.at[off],
               peer_chip(off) * 2 + par)
        for off in range(1, nc)
    ]
    pending.extend(loss_copies)

    gper = step_rows // (2 * gr)
    rows = resid[...].reshape(members * tok, dm)
    for i in range(dm // step_rows):
        part = dot_tn(rows[:, i * step_rows:(i + 1) * step_rows], dpred[...])
        g_f[i * gper:(i + 1) * gper] = part.reshape(gper, 2, gr, -1)

    def query_grad_step(step, held):
        for u in range(unroll):
            h = step * unroll + u
            for m in range(members):
                c = m * heads + h
                p = probs[c]
                dp = dot_nt(da[1, m, :, cols(h)], window(vw, v, m, h))
                delta = jnp.sum(p * dp, axis=-1, keepdims=True)
                ds = (p * (dp - delta) * scaling).astype(BF16)
                dq_o[m, :, cols(h)] = dot_nn(ds, window(kw, k, m, h)).astype(BF16)
                held = jnp.where(lane == members * heads + c, delta, held)
        return held

    stats[...] = lax.fori_loop(0, heads // unroll, query_grad_step, lse)
    halo_s = halo(5, stats, stw)
    write(dq_o, dq_out)

    for copy in ap_copies:
        copy.wait_recv()
    ap_total = ap_f[chip, par] + ap_r1[chip].astype(F32)
    for off in range(1, nc):
        ap_total = ap_total + ap_r2[off].astype(F32)
    ap_high = ap_total.astype(BF16)
    for i in range(dm // step_rows):
        part = dot_tn(w_out[:, i * step_rows:(i + 1) * step_rows], ap_high)
        part = g_f[i * gper:(i + 1) * gper] + part.reshape(gper, 2, gr, -1)
        g_f[i * gper:(i + 1) * gper] = part
        g_b[i * gper:(i + 1) * gper] = part.astype(BF16)
    g_pair = remote(g_b.at[:, 1 - par], g_r1, sib_ss.at[3], sib_rs.at[3], sib)
    pending.append(g_pair)
    ap_low = (ap_total - ap_high.astype(F32)).astype(BF16)
    dwo_o[...] = dot_nt(ap_high, w_head[...]) + dot_nt(ap_low, w_head[...])
    write(dwo_o, dwo_out)
    g_pair.wait_recv()
    g_copies = []
    for off in range(1, nc):
        c = peer_chip(off)
        g_s2[c] = (g_f[c, par] + g_r1[c].astype(F32)).astype(BF16)
        g_copies.append(
            remote(g_s2.at[c], g_r2.at[off], g_ss.at[off], g_rs.at[off], c * 2 + par)
        )
    pending.extend(g_copies)

    for copy in halo_d:
        copy.wait_recv()
    for side, place in ((0, 0), (1, 2)):
        da[place] = dot_nt(dpw[side], m_full).astype(BF16).reshape(members, tok, hd)
    for copy in halo_q + halo_s:
        copy.wait_recv()
    stat_window = jnp.concatenate([stw[0], stats[...], stw[1]], axis=0)
    count = stats_t.shape[0]
    eye = jnp.where(
        lax.broadcasted_iota(jnp.int32, (count, DH), 0)
        == lax.broadcasted_iota(jnp.int32, (count, DH), 1), 1.0, 0.0
    )
    stats_t[...] = dot_nt(eye, stat_window, lax.Precision.HIGHEST)

    def key_grad_step(step, _):
        for u in range(unroll):
            h = step * unroll + u
            for m in range(members):
                c = m * heads + h
                queries = window(qw, q, m, h)
                grads = jnp.concatenate([da[i, m, :, cols(h)] for i in range(3)], axis=0)
                s = dot_nt(k[m, :, cols(h)], queries) * scaling + bias[...]
                p = jnp.exp(s - stats_t[pl.ds(c, 1), :])
                dp = dot_nt(v[m, :, cols(h)], grads)
                ds = (p * (dp - stats_t[pl.ds(members * heads + c, 1), :]) * scaling).astype(BF16)
                dv_o[m, :, cols(h)] = dot_nn(p.astype(BF16), grads).astype(BF16)
                dk_o[m, :, cols(h)] = dot_nn(ds, queries).astype(BF16)
        return 0

    lax.fori_loop(0, heads // unroll, key_grad_step, 0)
    write(dk_o, dk_out)
    write(dv_o, dv_out)

    for copy in g_copies:
        copy.wait_recv()
    g_total = g_f[chip, par] + g_r1[chip].astype(F32)
    for off in range(1, nc):
        g_total = g_total + g_r2[off].astype(F32)
    dwh_o[chip, par] = g_total.astype(BF16)
    outer_count = nc // 2
    row, col = chip // 2, chip % 2
    across = (row * 2 + 1 - col) * 2 + par
    forwards, along, over = [], [], []

    def send_on(c, off, to_across):
        block = dwh_o.at[c, par]
        if to_across:
            over.append(
                remote(block, block, ag_ss.at[outer_count + off], ag_rs.at[outer_count + off], across)
            )
        place = off if to_across else outer_count + off
        forwards.append(remote(block, block, fw_ss.at[place], fw_rs.at[place], sib))

    own = dwh_o.at[chip, par]
    for off in range(1, outer_count):
        to = (lax.rem(row + off, outer_count) * 2 + col) * 2 + par
        along.append(remote(own, own, ag_ss.at[off], ag_rs.at[off], to))
    send_on(chip, 0, True)
    for copy in loss_copies:
        copy.wait_recv()
    loss_o[...] = jnp.sum(loss_all[...], axis=0) / (n * tok * dpred.shape[1])
    write(loss_o, loss_out)
    for off in range(1, outer_count):
        along[off - 1].wait_recv()
        send_on(lax.rem(row + outer_count - off, outer_count) * 2 + col, off, True)
    for off in range(outer_count):
        over[off].wait_recv()
        send_on(lax.rem(row + outer_count - off, outer_count) * 2 + 1 - col, off, False)
    pending.extend(along + over)
    for copy in forwards:
        copy.wait_recv()
    write(dwh_o, dwh_out)
    for copy in pending + forwards:
        copy.wait_send()
    for copy in written:
        copy.wait()


def finish(loss, dq, dk, dv, dwo, dwh, loss_o, dq_o, dk_o, dv_o, dwo_o, dwh_o,
           loss_v, dq_v, dk_v, dv_v, dwo_v, half, wide, sem):
    parts = wide.shape[0]
    plain = ((dwo, dwo_v, dwo_o), (dq, dq_v, dq_o), (dk, dk_v, dk_o), (dv, dv_v, dv_o))
    load = [pltpu.make_async_copy(dwh.at[i], half.at[i], sem.at[i]) for i in range(parts)]
    load += [
        pltpu.make_async_copy(src, mid, sem.at[parts + i]) for i, (src, mid, _) in enumerate(plain)
    ]
    load.append(pltpu.make_async_copy(loss, loss_v, sem.at[parts + 4]))
    for copy in load:
        copy.start()
    stores = []

    def store(src, dst):
        copy = pltpu.make_async_copy(src, dst, sem.at[parts + 5 + len(stores)])
        copy.start()
        stores.append(copy)

    for i in range(parts):
        load[i].wait()
        wide[i] = half[i].astype(F32)
        store(wide.at[i], dwh_o.at[i])
    for i, (_, mid, dst) in enumerate(plain):
        load[parts + i].wait()
        store(mid, dst)
    load[parts + 4].wait()
    loss_o[0] = loss_v[0, 0]
    for copy in stores:
        copy.wait()


def per_device(queries, keys, values, resid, w_out, w_head, target, block_ids):
    members, tok, hd = queries.shape
    heads = hd // DH
    n = lax.axis_size("seq")
    nc = n // 2
    dm, width = w_head.shape
    ar, gr = hd // n, dm // n
    ids = block_ids.reshape(1, tok)
    hbm = pl.BlockSpec(memory_space=pltpu.HBM)
    dma = pltpu.SemaphoreType.DMA
    like = jax.ShapeDtypeStruct(queries.shape, BF16)
    results = pl.pallas_call(
        functools.partial(kernel, n),
        out_shape=(
            jax.ShapeDtypeStruct((8, DH), F32),
            like, like, like,
            jax.ShapeDtypeStruct((ar, dm), F32),
            jax.ShapeDtypeStruct((nc, 2, gr, width), BF16),
        ),
        in_specs=[hbm] * 8,
        out_specs=(hbm,) * 6,
        scratch_shapes=[
            pltpu.VMEM((8, DH), F32),
            pltpu.VMEM(queries.shape, BF16),
            pltpu.VMEM(queries.shape, BF16),
            pltpu.VMEM(queries.shape, BF16),
            pltpu.VMEM((ar, dm), F32),
            pltpu.VMEM((nc, 2, gr, width), BF16),
            dma((6,)),
            pltpu.VMEM(queries.shape, BF16),
            pltpu.VMEM(queries.shape, BF16),
            pltpu.VMEM(queries.shape, BF16),
            pltpu.VMEM(resid.shape, BF16),
            pltpu.VMEM(w_out.shape, BF16),
            pltpu.VMEM(w_head.shape, BF16),
            pltpu.VMEM(target.shape, F32),
            pltpu.VMEM((1, tok), jnp.int32),
            pltpu.VMEM((tok, DH), BF16),
            dma((8,)),
            pltpu.VMEM((2,) + keys.shape, BF16),
            pltpu.VMEM((2,) + keys.shape, BF16),
            pltpu.VMEM((2,) + keys.shape, BF16),
            pltpu.VMEM((2, tok, DH), BF16),
            pltpu.VMEM((2, members * tok, width), BF16),
            pltpu.VMEM((2, tok, DH), F32),
            pltpu.VMEM((nc, 2, ar, width), BF16),
            pltpu.VMEM((members * tok, width), F32),
            pltpu.VMEM((tok, 3 * tok), F32),
            pltpu.VMEM((members * heads, tok, 3 * tok), F32),
            pltpu.VMEM(queries.shape, BF16),
            pltpu.VMEM((members * tok, width), BF16),
            pltpu.VMEM((3,) + queries.shape, BF16),
            pltpu.VMEM((tok, DH), F32),
            pltpu.VMEM((2 * members * heads, 3 * tok), F32),
            pltpu.VMEM((nc, 2, ar, width), F32),
            pltpu.VMEM((nc, 2, ar, width), BF16),
            pltpu.VMEM((nc, ar, width), BF16),
            pltpu.VMEM((nc, ar, width), BF16),
            pltpu.VMEM((nc, ar, width), BF16),
            pltpu.VMEM((nc, 2, gr, width), F32),
            pltpu.VMEM((nc, 2, gr, width), BF16),
            pltpu.VMEM((nc, gr, width), BF16),
            pltpu.VMEM((nc, gr, width), BF16),
            pltpu.VMEM((nc, gr, width), BF16),
            pltpu.VMEM((8, DH), F32),
            pltpu.VMEM((8, DH), F32),
            pltpu.VMEM((nc, 8, DH), F32),
            dma((12,)), dma((12,)),
            dma((nc,)), dma((nc,)),
            dma((4,)), dma((4,)),
            dma((nc,)), dma((nc,)),
            dma((nc,)), dma((nc,)),
            dma((nc,)), dma((nc,)),
            dma((nc,)), dma((nc,)),
            dma((nc,)), dma((nc,)),
        ],
        compiler_params=pltpu.CompilerParams(
            collective_id=0, has_side_effects=True, vmem_limit_bytes=60 * 1024 * 1024
        ),
        cost_estimate=pl.CostEstimate(
            flops=2_000_000_000, bytes_accessed=6_000_000, transcendentals=1_000_000
        ),
    )(queries, keys, values, resid, w_out, w_head, target, ids)
    parts = 4
    rows = dm // parts
    loss, d_queries, d_keys, d_values, d_w_out, d_w_head = pl.pallas_call(
        finish,
        out_shape=(
            jax.ShapeDtypeStruct((1,), F32),
            like, like, like,
            jax.ShapeDtypeStruct((ar, dm), F32),
            jax.ShapeDtypeStruct((parts, rows, width), F32),
        ),
        in_specs=[hbm] * 6,
        out_specs=(pl.BlockSpec(memory_space=pltpu.SMEM),) + (hbm,) * 5,
        scratch_shapes=[
            pltpu.VMEM((8, DH), F32),
            pltpu.VMEM(queries.shape, BF16),
            pltpu.VMEM(queries.shape, BF16),
            pltpu.VMEM(queries.shape, BF16),
            pltpu.VMEM((ar, dm), F32),
            pltpu.VMEM((parts, rows, width), BF16),
            pltpu.VMEM((parts, rows, width), F32),
            dma((9 + 2 * parts,)),
        ],
        compiler_params=pltpu.CompilerParams(vmem_limit_bytes=60 * 1024 * 1024),
        cost_estimate=pl.CostEstimate(flops=1_000_000, bytes_accessed=6_000_000, transcendentals=0),
    )(*results[:5], results[5].reshape(parts, rows, width))
    return (loss, d_queries, d_keys, d_values, d_w_out, d_w_head.reshape(dm, width))


def solution(mesh):
    return jax.shard_map(
        per_device,
        mesh=mesh,
        in_specs=(
            P("groups", "seq", None),
            P("groups", "seq", None),
            P("groups", "seq", None),
            P("groups", "seq", None),
            P("seq", None),
            P(),
            P(("groups", "seq"), None),
            P(("groups", "seq")),
        ),
        out_specs=(
            P("groups"),
            P("groups", "seq", None),
            P("groups", "seq", None),
            P("groups", "seq", None),
            P(("groups", "seq"), None),
            P("groups", None),
        ),
        check_vma=False,
    )
```

```python
import functools

import jax
import jax.numpy as jnp
from jax import lax
from jax.experimental import pallas as pl
from jax.experimental.pallas import tpu as pltpu
from jax.sharding import PartitionSpec as P

DH = 128
F32 = jnp.float32
BF16 = jnp.bfloat16


def dot_nn(a, b):
    return lax.dot_general(a, b, (((1,), (0,)), ((), ())), preferred_element_type=F32)


def dot_nt(a, b, precision=None):
    return lax.dot_general(
        a, b, (((1,), (1,)), ((), ())), preferred_element_type=F32, precision=precision
    )


def dot_tn(a, b):
    return lax.dot_general(a, b, (((0,), (0,)), ((), ())), preferred_element_type=F32)


def kernel(
    n,
    q_in, k_in, v_in, resid_in, w_out_in, w_head_in, target_in, ids_in,
    loss_out, dq_out, dk_out, dv_out, dwo_out, dwh_out,
    loss_o, dq_o, dk_o, dv_o, dwo_o, dwh_o, out_sem,
    q, k, v, resid, w_out, w_head, target, id_row, ids, in_sem,
    kw, vw, qw, idw, dpw, stw,
    m_all, pred0, bias, probs, att, dpred, da, stats, stats_t,
    ap_f, ap_b, ap_r1, ap_s2, ap_r2,
    g_f, g_b, g_r1, g_s2, g_r2,
    loss_own, loss_sib, loss_all,
    halo_ss, halo_rs, m_ss, m_rs, sib_ss, sib_rs, ap_ss, ap_rs, g_ss, g_rs,
    ag_ss, ag_rs, fw_ss, fw_rs, lo_ss, lo_rs,
):
    members, tok, hd = q.shape
    heads = hd // DH
    dm = resid.shape[2]
    nc = n // 2
    ar = hd // n
    gr = dm // n
    scaling = DH ** (-0.5)
    me = lax.axis_index("seq")
    chip, par = me // 2, me % 2
    sib = chip * 2 + (1 - par)
    left, right = lax.rem(me + n - 1, n), lax.rem(me + 1, n)
    outer = lax.rem(me + n - 1 + 2 * par, n)

    def peer_chip(off):
        return lax.rem(chip + off, nc)

    def source_chip(off):
        return lax.rem(chip + nc - off, nc)

    def remote(src, dst, ss, rs, to):
        copy = pltpu.make_async_remote_copy(
            src_ref=src, dst_ref=dst, send_sem=ss, recv_sem=rs,
            device_id={"seq": to}, device_id_type=pl.DeviceIdType.MESH,
        )
        copy.start()
        return copy

    local = [
        pltpu.make_async_copy(src, dst, in_sem.at[i])
        for i, (src, dst) in enumerate((
            (ids_in, id_row), (w_head_in, w_head), (w_out_in, w_out), (k_in, k), (resid_in, resid),
            (q_in, q), (v_in, v), (target_in, target),
        ))
    ]
    for copy in local:
        copy.start()

    written = []

    def write(src, dst):
        copy = pltpu.make_async_copy(src, dst, out_sem.at[len(written)])
        copy.start()
        written.append(copy)

    barrier = pltpu.get_barrier_semaphore()
    for to in [sib, outer] + [peer_chip(off) * 2 + par for off in range(1, nc)]:
        pl.semaphore_signal(
            barrier, inc=1, device_id={"seq": to}, device_id_type=pl.DeviceIdType.MESH
        )
    local[0].wait()
    square = (tok, tok)
    diagonal = lax.broadcasted_iota(jnp.int32, square, 0) == lax.broadcasted_iota(jnp.int32, square, 1)
    id_column = jnp.sum(
        jnp.where(diagonal, id_row[...].astype(F32), 0.0), axis=1, keepdims=True
    )
    ids[...] = jnp.broadcast_to(id_column, ids.shape).astype(BF16)
    pl.semaphore_wait(barrier, nc + 1)

    pending = []

    def halo(slot, src, dst):
        pair = (
            remote(src, dst.at[0], halo_ss.at[2 * slot], halo_rs.at[2 * slot], right),
            remote(src, dst.at[1], halo_ss.at[2 * slot + 1], halo_rs.at[2 * slot + 1], left),
        )
        pending.extend(pair)
        return pair

    halo_id = halo(0, ids, idw)
    halo_k = halo(1, k_in, kw)
    halo_v = halo(2, v_in, vw)
    local[1].wait()
    local[2].wait()

    m_all[chip, par] = dot_nn(w_out[...], w_head[...]).astype(BF16)
    m_copies = [
        remote(m_all.at[chip, par], m_all.at[chip, par], m_ss.at[off], m_rs.at[off],
               peer_chip(off) * 2 + par)
        for off in range(1, nc)
    ]
    pending.extend(m_copies)
    for copy in local[3:]:
        copy.wait()

    pred0[...] = dot_nn(resid[...].reshape(members * tok, dm), w_head[...])

    for copy in halo_id + halo_k:
        copy.wait_recv()
    id_window = jnp.concatenate([idw[0], ids[...], idw[1]], axis=0)
    lane = lax.broadcasted_iota(jnp.int32, (tok, DH), 1)
    first = jnp.where(lane == 0, 1.0, 0.0).astype(BF16)
    window_ids = dot_nt(first, id_window)
    own_ids = ids[...].astype(F32)[:, 0:1]
    gap = jnp.abs(own_ids - window_ids)
    number = 4.0 * n
    bias[...] = jnp.where((gap < 1.5) | (gap > number - 1.5), 0.0, -1e30)

    def cols(h):
        return pl.ds(pl.multiple_of(h * DH, DH), DH)

    def window(side, own, m, h):
        return jnp.concatenate(
            [side[0, m, :, cols(h)], own[m, :, cols(h)], side[1, m, :, cols(h)]], axis=0
        )

    unroll = 2

    def softmax_step(step, held):
        for u in range(unroll):
            h = step * unroll + u
            for m in range(members):
                c = m * heads + h
                s = dot_nt(q[m, :, cols(h)], window(kw, k, m, h)) * scaling + bias[...]
                peak = jnp.max(s, axis=-1, keepdims=True)
                e = jnp.exp(s - peak)
                total = jnp.sum(e, axis=-1, keepdims=True)
                probs[c] = e / total
                held = jnp.where(lane == c, peak + jnp.log(total), held)
        return held

    lse = lax.fori_loop(0, heads // unroll, softmax_step, jnp.zeros((tok, DH), F32))

    for copy in m_copies:
        copy.wait_recv()
    m_forward = remote(m_all.at[:, par], m_all.at[:, par], sib_ss.at[0], sib_rs.at[0], sib)
    pending.append(m_forward)
    for copy in halo_v:
        copy.wait_recv()
    halo_q = halo(3, q_in, qw)

    def attend_step(step, _):
        for u in range(unroll):
            h = step * unroll + u
            for m in range(members):
                p = probs[m * heads + h].astype(BF16)
                att[m, :, cols(h)] = dot_nn(p, window(vw, v, m, h)).astype(BF16)
        return 0

    lax.fori_loop(0, heads // unroll, attend_step, 0)

    m_forward.wait_recv()
    attended = att[...].reshape(members * tok, hd)
    m_full = m_all[...].reshape(hd, -1)
    predicted = pred0[...] + dot_nn(attended, m_full)
    p0, p1 = predicted[:tok], predicted[tok:]
    o0, o1, pair = p0 - target[...], p1 - target[...], p0 - p1
    s0 = jnp.sqrt(1.0 + o0 * o0)
    s1 = jnp.sqrt(1.0 + o1 * o1)
    sp = jnp.sqrt(1.0 + pair * pair)
    score = 0.5 * ((s0 - 1.0) + (s1 - 1.0)) - 0.5 * (sp - 1.0)
    shared = 0.5 * (pair / sp)
    dpred[0:tok] = (0.5 * (o0 / s0) - shared).astype(BF16)
    dpred[tok:] = (0.5 * (o1 / s1) + shared).astype(BF16)
    halo_d = halo(4, dpred, dpw)

    step_rows = 256
    per = step_rows // (2 * ar)
    for i in range(hd // step_rows):
        part = dot_tn(attended[:, i * step_rows:(i + 1) * step_rows], dpred[...])
        part = part.reshape(per, 2, ar, -1)
        ap_f[i * per:(i + 1) * per] = part
        ap_b[i * per:(i + 1) * per] = part.astype(BF16)
    ap_pair = remote(ap_b.at[:, 1 - par], ap_r1, sib_ss.at[1], sib_rs.at[1], sib)
    pending.append(ap_pair)

    loss_own[...] = jnp.broadcast_to(jnp.sum(score).reshape(1, 1), loss_own.shape)
    loss_pair = remote(loss_own, loss_sib, sib_ss.at[2], sib_rs.at[2], sib)
    pending.append(loss_pair)

    da[1] = dot_nt(dpred[...], m_full).astype(BF16).reshape(members, tok, hd)

    ap_pair.wait_recv()
    ap_copies = []
    for off in range(1, nc):
        c = peer_chip(off)
        ap_s2[c] = (ap_f[c, par] + ap_r1[c].astype(F32)).astype(BF16)
        ap_copies.append(
            remote(ap_s2.at[c], ap_r2.at[off], ap_ss.at[off], ap_rs.at[off], c * 2 + par)
        )
    pending.extend(ap_copies)
    loss_pair.wait_recv()
    loss_all[chip] = loss_own[...] + loss_sib[...]
    loss_copies = [
        remote(loss_all.at[chip], loss_all.at[chip], lo_ss.at[off], lo_rs.at[off],
               peer_chip(off) * 2 + par)
        for off in range(1, nc)
    ]
    pending.extend(loss_copies)

    gper = step_rows // (2 * gr)
    rows = resid[...].reshape(members * tok, dm)
    for i in range(dm // step_rows):
        part = dot_tn(rows[:, i * step_rows:(i + 1) * step_rows], dpred[...])
        g_f[i * gper:(i + 1) * gper] = part.reshape(gper, 2, gr, -1)

    def query_grad_step(step, held):
        for u in range(unroll):
            h = step * unroll + u
            for m in range(members):
                c = m * heads + h
                p = probs[c]
                dp = dot_nt(da[1, m, :, cols(h)], window(vw, v, m, h))
                delta = jnp.sum(p * dp, axis=-1, keepdims=True)
                ds = (p * (dp - delta) * scaling).astype(BF16)
                dq_o[m, :, cols(h)] = dot_nn(ds, window(kw, k, m, h)).astype(BF16)
                held = jnp.where(lane == members * heads + c, delta, held)
        return held

    stats[...] = lax.fori_loop(0, heads // unroll, query_grad_step, lse)
    halo_s = halo(5, stats, stw)
    write(dq_o, dq_out)

    for copy in ap_copies:
        copy.wait_recv()
    ap_total = ap_f[chip, par] + ap_r1[chip].astype(F32)
    for off in range(1, nc):
        ap_total = ap_total + ap_r2[off].astype(F32)
    ap_high = ap_total.astype(BF16)
    for i in range(dm // step_rows):
        part = dot_tn(w_out[:, i * step_rows:(i + 1) * step_rows], ap_high)
        part = g_f[i * gper:(i + 1) * gper] + part.reshape(gper, 2, gr, -1)
        g_f[i * gper:(i + 1) * gper] = part
        g_b[i * gper:(i + 1) * gper] = part.astype(BF16)
    g_pair = remote(g_b.at[:, 1 - par], g_r1, sib_ss.at[3], sib_rs.at[3], sib)
    pending.append(g_pair)
    ap_low = (ap_total - ap_high.astype(F32)).astype(BF16)
    dwo_o[...] = dot_nt(ap_high, w_head[...]) + dot_nt(ap_low, w_head[...])
    write(dwo_o, dwo_out)
    g_pair.wait_recv()
    g_copies = []
    for off in range(1, nc):
        c = peer_chip(off)
        g_s2[c] = (g_f[c, par] + g_r1[c].astype(F32)).astype(BF16)
        g_copies.append(
            remote(g_s2.at[c], g_r2.at[off], g_ss.at[off], g_rs.at[off], c * 2 + par)
        )
    pending.extend(g_copies)

    for copy in halo_d:
        copy.wait_recv()
    for side, place in ((0, 0), (1, 2)):
        da[place] = dot_nt(dpw[side], m_full).astype(BF16).reshape(members, tok, hd)
    for copy in halo_q + halo_s:
        copy.wait_recv()
    stat_window = jnp.concatenate([stw[0], stats[...], stw[1]], axis=0)
    count = stats_t.shape[0]
    eye = jnp.where(
        lax.broadcasted_iota(jnp.int32, (count, DH), 0)
        == lax.broadcasted_iota(jnp.int32, (count, DH), 1), 1.0, 0.0
    )
    stats_t[...] = dot_nt(eye, stat_window, lax.Precision.HIGHEST)

    def key_grad_step(step, _):
        for u in range(unroll):
            h = step * unroll + u
            for m in range(members):
                c = m * heads + h
                queries = window(qw, q, m, h)
                grads = jnp.concatenate([da[i, m, :, cols(h)] for i in range(3)], axis=0)
                s = dot_nt(k[m, :, cols(h)], queries) * scaling + bias[...]
                p = jnp.exp(s - stats_t[pl.ds(c, 1), :])
                dp = dot_nt(v[m, :, cols(h)], grads)
                ds = (p * (dp - stats_t[pl.ds(members * heads + c, 1), :]) * scaling).astype(BF16)
                dv_o[m, :, cols(h)] = dot_nn(p.astype(BF16), grads).astype(BF16)
                dk_o[m, :, cols(h)] = dot_nn(ds, queries).astype(BF16)
        return 0

    lax.fori_loop(0, heads // unroll, key_grad_step, 0)
    write(dk_o, dk_out)
    write(dv_o, dv_out)

    for copy in g_copies:
        copy.wait_recv()
    g_total = g_f[chip, par] + g_r1[chip].astype(F32)
    for off in range(1, nc):
        g_total = g_total + g_r2[off].astype(F32)
    dwh_o[chip, par] = g_total.astype(BF16)
    outer_count = nc // 2
    row, col = chip // 2, chip % 2
    across = (row * 2 + 1 - col) * 2 + par
    forwards, along, over = [], [], []

    split = 2
    piece = gr // split

    def block_of(c, part):
        return dwh_o.at[c, par, pl.ds(part * piece, piece)]

    def send_on(c, off, part, to_across):
        block = block_of(c, part)
        if to_across:
            at = (outer_count + off) * split + part
            over.append(remote(block, block, ag_ss.at[at], ag_rs.at[at], across))
        at = (off if to_across else outer_count + off) * split + part
        forwards.append(remote(block, block, fw_ss.at[at], fw_rs.at[at], sib))

    for part in range(split):
        own = block_of(chip, part)
        for off in range(1, outer_count):
            to = (lax.rem(row + off, outer_count) * 2 + col) * 2 + par
            at = off * split + part
            along.append(remote(own, own, ag_ss.at[at], ag_rs.at[at], to))
    for part in range(split):
        send_on(chip, 0, part, True)
    for copy in loss_copies:
        copy.wait_recv()
    loss_o[...] = jnp.sum(loss_all[...], axis=0) / (n * tok * dpred.shape[1])
    write(loss_o, loss_out)
    arrived = iter(along)
    for part in range(split):
        for off in range(1, outer_count):
            next(arrived).wait_recv()
            send_on(
                lax.rem(row + outer_count - off, outer_count) * 2 + col, off, part, True
            )
    arrived = iter(list(over))
    for off, part in [(0, part) for part in range(split)] + [
        (off, part) for part in range(split) for off in range(1, outer_count)
    ]:
        next(arrived).wait_recv()
        send_on(
            lax.rem(row + outer_count - off, outer_count) * 2 + 1 - col, off, part, False
        )
    pending.extend(along + over)
    for copy in forwards:
        copy.wait_recv()
    write(dwh_o, dwh_out)
    for copy in pending + forwards:
        copy.wait_send()
    for copy in written:
        copy.wait()


def finish(loss, dq, dk, dv, dwo, dwh, loss_o, dq_o, dk_o, dv_o, dwo_o, dwh_o,
           loss_v, dq_v, dk_v, dv_v, dwo_v, half, wide, sem):
    parts = wide.shape[0]
    plain = ((dwo, dwo_v, dwo_o), (dq, dq_v, dq_o), (dk, dk_v, dk_o), (dv, dv_v, dv_o))
    load = [pltpu.make_async_copy(dwh.at[i], half.at[i], sem.at[i]) for i in range(parts)]
    load += [
        pltpu.make_async_copy(src, mid, sem.at[parts + i]) for i, (src, mid, _) in enumerate(plain)
    ]
    load.append(pltpu.make_async_copy(loss, loss_v, sem.at[parts + 4]))
    for copy in load:
        copy.start()
    stores = []

    def store(src, dst):
        copy = pltpu.make_async_copy(src, dst, sem.at[parts + 5 + len(stores)])
        copy.start()
        stores.append(copy)

    for i in range(parts):
        load[i].wait()
        wide[i] = half[i].astype(F32)
        store(wide.at[i], dwh_o.at[i])
    for i, (_, mid, dst) in enumerate(plain):
        load[parts + i].wait()
        store(mid, dst)
    load[parts + 4].wait()
    loss_o[0] = loss_v[0, 0]
    for copy in stores:
        copy.wait()


def per_device(queries, keys, values, resid, w_out, w_head, target, block_ids):
    members, tok, hd = queries.shape
    heads = hd // DH
    n = lax.axis_size("seq")
    nc = n // 2
    dm, width = w_head.shape
    ar, gr = hd // n, dm // n
    ids = block_ids.reshape(1, tok)
    hbm = pl.BlockSpec(memory_space=pltpu.HBM)
    dma = pltpu.SemaphoreType.DMA
    like = jax.ShapeDtypeStruct(queries.shape, BF16)
    results = pl.pallas_call(
        functools.partial(kernel, n),
        out_shape=(
            jax.ShapeDtypeStruct((8, DH), F32),
            like, like, like,
            jax.ShapeDtypeStruct((ar, dm), F32),
            jax.ShapeDtypeStruct((nc, 2, gr, width), BF16),
        ),
        in_specs=[hbm] * 8,
        out_specs=(hbm,) * 6,
        scratch_shapes=[
            pltpu.VMEM((8, DH), F32),
            pltpu.VMEM(queries.shape, BF16),
            pltpu.VMEM(queries.shape, BF16),
            pltpu.VMEM(queries.shape, BF16),
            pltpu.VMEM((ar, dm), F32),
            pltpu.VMEM((nc, 2, gr, width), BF16),
            dma((6,)),
            pltpu.VMEM(queries.shape, BF16),
            pltpu.VMEM(queries.shape, BF16),
            pltpu.VMEM(queries.shape, BF16),
            pltpu.VMEM(resid.shape, BF16),
            pltpu.VMEM(w_out.shape, BF16),
            pltpu.VMEM(w_head.shape, BF16),
            pltpu.VMEM(target.shape, F32),
            pltpu.VMEM((1, tok), jnp.int32),
            pltpu.VMEM((tok, DH), BF16),
            dma((8,)),
            pltpu.VMEM((2,) + keys.shape, BF16),
            pltpu.VMEM((2,) + keys.shape, BF16),
            pltpu.VMEM((2,) + keys.shape, BF16),
            pltpu.VMEM((2, tok, DH), BF16),
            pltpu.VMEM((2, members * tok, width), BF16),
            pltpu.VMEM((2, tok, DH), F32),
            pltpu.VMEM((nc, 2, ar, width), BF16),
            pltpu.VMEM((members * tok, width), F32),
            pltpu.VMEM((tok, 3 * tok), F32),
            pltpu.VMEM((members * heads, tok, 3 * tok), F32),
            pltpu.VMEM(queries.shape, BF16),
            pltpu.VMEM((members * tok, width), BF16),
            pltpu.VMEM((3,) + queries.shape, BF16),
            pltpu.VMEM((tok, DH), F32),
            pltpu.VMEM((2 * members * heads, 3 * tok), F32),
            pltpu.VMEM((nc, 2, ar, width), F32),
            pltpu.VMEM((nc, 2, ar, width), BF16),
            pltpu.VMEM((nc, ar, width), BF16),
            pltpu.VMEM((nc, ar, width), BF16),
            pltpu.VMEM((nc, ar, width), BF16),
            pltpu.VMEM((nc, 2, gr, width), F32),
            pltpu.VMEM((nc, 2, gr, width), BF16),
            pltpu.VMEM((nc, gr, width), BF16),
            pltpu.VMEM((nc, gr, width), BF16),
            pltpu.VMEM((nc, gr, width), BF16),
            pltpu.VMEM((8, DH), F32),
            pltpu.VMEM((8, DH), F32),
            pltpu.VMEM((nc, 8, DH), F32),
            dma((12,)), dma((12,)),
            dma((nc,)), dma((nc,)),
            dma((4,)), dma((4,)),
            dma((nc,)), dma((nc,)),
            dma((nc,)), dma((nc,)),
            dma((2 * nc,)), dma((2 * nc,)),
            dma((2 * nc,)), dma((2 * nc,)),
            dma((nc,)), dma((nc,)),
        ],
        compiler_params=pltpu.CompilerParams(
            collective_id=0, has_side_effects=True, vmem_limit_bytes=60 * 1024 * 1024
        ),
        cost_estimate=pl.CostEstimate(
            flops=2_000_000_000, bytes_accessed=6_000_000, transcendentals=1_000_000
        ),
    )(queries, keys, values, resid, w_out, w_head, target, ids)
    parts = 4
    rows = dm // parts
    loss, d_queries, d_keys, d_values, d_w_out, d_w_head = pl.pallas_call(
        finish,
        out_shape=(
            jax.ShapeDtypeStruct((1,), F32),
            like, like, like,
            jax.ShapeDtypeStruct((ar, dm), F32),
            jax.ShapeDtypeStruct((parts, rows, width), F32),
        ),
        in_specs=[hbm] * 6,
        out_specs=(pl.BlockSpec(memory_space=pltpu.SMEM),) + (hbm,) * 5,
        scratch_shapes=[
            pltpu.VMEM((8, DH), F32),
            pltpu.VMEM(queries.shape, BF16),
            pltpu.VMEM(queries.shape, BF16),
            pltpu.VMEM(queries.shape, BF16),
            pltpu.VMEM((ar, dm), F32),
            pltpu.VMEM((parts, rows, width), BF16),
            pltpu.VMEM((parts, rows, width), F32),
            dma((9 + 2 * parts,)),
        ],
        compiler_params=pltpu.CompilerParams(vmem_limit_bytes=60 * 1024 * 1024),
        cost_estimate=pl.CostEstimate(flops=1_000_000, bytes_accessed=6_000_000, transcendentals=0),
    )(*results[:5], results[5].reshape(parts, rows, width))
    return (loss, d_queries, d_keys, d_values, d_w_out, d_w_head.reshape(dm, width))


def solution(mesh):
    return jax.shard_map(
        per_device,
        mesh=mesh,
        in_specs=(
            P("groups", "seq", None),
            P("groups", "seq", None),
            P("groups", "seq", None),
            P("groups", "seq", None),
            P("seq", None),
            P(),
            P(("groups", "seq"), None),
            P(("groups", "seq")),
        ),
        out_specs=(
            P("groups"),
            P("groups", "seq", None),
            P("groups", "seq", None),
            P("groups", "seq", None),
            P(("groups", "seq"), None),
            P("groups", None),
        ),
        check_vma=False,
    )
```
